32 devices in a mesh: dp: 4 (over y, core), row: 2 (over x), col: 4 (over z).
Axes of the slice: x: 2, y: 2, z: 4, core: 2. Of those that a mesh axis runs over, the one named last changes fastest.
Arguments:
- x_in: bfloat16 [4096, 2048], P(('dp', 'row'), 'col'), may hold values from -6 to 6
- seq_lens: int32 [16], replicated, may hold values from 1 to 1024, as said below
- seq_groups: int32 [16], replicated, may hold values from 0 to 3, as said below
- ln1_gain: float32 [2048], P('col'), may hold values from 0.5 to 1.5
- ln1_bias: float32 [2048], P('col'), may hold values from -1.5 to 1.5
- w_query: bfloat16 [2048, 2048], P('row', 'col'), may hold values from -0.125 to 0.125
- w_key: bfloat16 [2048, 2048], P('row', 'col'), may hold values from -0.125 to 0.125
- w_value: bfloat16 [4096, 2048], P('row', 'col'), may hold values from -0.125 to 0.125
- w_swish: bfloat16 [4096, 2048], P('row', 'col'), may hold values from -0.125 to 0.125
- gn_gain: float32 [4096], P(('row', 'col')), may hold values from 0.5 to 1.5
- w_out: bfloat16 [2048, 4096], P('col', 'row'), may hold values from -0.09375 to 0.09375
- ln2_gain: float32 [2048], P('col'), may hold values from 0.5 to 1.5
- ln2_bias: float32 [2048], P('col'), may hold values from -1.5 to 1.5
- w_mlp_gate: bfloat16 [4096, 2048], P('row', 'col'), may hold values from -0.125 to 0.125
- w_mlp_up: bfloat16 [4096, 2048], P('row', 'col'), may hold values from -0.125 to 0.125
- w_down: bfloat16 [2048, 4096], P('col', 'row'), may hold values from -0.09375 to 0.09375
- d_out: bfloat16 [4096, 2048], P(('dp', 'row'), 'col'), may hold values from -6 to 6
Outputs:
- y_out: float32 [4096, 2048], P(('dp', 'row'), 'col')
- d_x_in: float32 [4096, 2048], P(('dp', 'row'), 'col')
- d_ln1_gain: float32 [2048], P('col')
- d_ln1_bias: float32 [2048], P('col')
- d_w_query: float32 [2048, 2048], P('row', 'col')
- d_w_key: float32 [2048, 2048], P('row', 'col')
- d_w_value: float32 [4096, 2048], P('row', 'col')
- d_w_swish: float32 [4096, 2048], P('row', 'col')
- d_gn_gain: float32 [4096], P(('row', 'col'))
- d_w_out: float32 [2048, 4096], P('col', 'row')
- d_ln2_gain: float32 [2048], P('col')
- d_ln2_bias: float32 [2048], P('col')
- d_w_mlp_gate: float32 [4096, 2048], P('row', 'col')
- d_w_mlp_up: float32 [4096, 2048], P('row', 'col')
- d_w_down: float32 [2048, 4096], P('col', 'row')
The draws below stay inside these ranges and needn't reach their ends.
Inputs may be any that keep to these rules, and one draw needn't show every extreme that they name: `seq_lens`: within each group the lengths sum to at most 1024; one group holds a single sequence of exactly 1024; the lowest-numbered sequence of each group is longer than 512. `seq_groups`: every group holds at least one sequence.
All inputs are finite; a program needn't handle non-finite values.
Results may differ from the reference program's by a relative error of at most 0.018.
Values may be sent and summed in bfloat16 or wider, within the bound.
A program may use at most 192 MiB of HBM per device.

```python
import math
import jax
import jax.numpy as jnp
from jax import lax

D = 2048
HEADS = 8
KD = 256
VH = 512
FF = 4096
CAP = 1024
QK = 2048
VDIM = 4096
NSEQ = 16
TOKENS = 4096
N_DP = 4


def sequence_plan(key):
    sub_keys = jax.random.split(key, 6)
    full_group = jax.random.randint(sub_keys[5], (), 0, N_DP, dtype=jnp.int32)
    ensured = jax.random.permutation(sub_keys[0], N_DP).astype(jnp.int32)
    raw_spread = jax.random.randint(sub_keys[1], (NSEQ - N_DP,), 0, N_DP - 1, dtype=jnp.int32)
    spread = jnp.where(raw_spread >= full_group, raw_spread + 1, raw_spread).astype(jnp.int32)
    shuffle = jax.random.permutation(sub_keys[2], NSEQ)
    groups = jnp.concatenate([ensured, spread])[shuffle].astype(jnp.int32)
    member = (groups[:, None] == jnp.arange(N_DP, dtype=jnp.int32)[None, :]).astype(jnp.int32)
    before = (jnp.cumsum(member, axis=0) - member).astype(jnp.int32)
    rank_in = jnp.sum(before * member, axis=1).astype(jnp.int32)
    counts = jnp.sum(member, axis=0).astype(jnp.int32)
    own_count = jnp.sum(member * counts[None, :], axis=1).astype(jnp.int32)
    spare_slots = CAP // 2 - 1
    others = jnp.maximum(own_count - 1, 1)
    extra_bound = (spare_slots - (own_count - 1)) // others
    extra_len = jax.random.randint(sub_keys[3], (NSEQ,), 0, extra_bound + 1, dtype=jnp.int32)
    later_len = jnp.where(rank_in > 0, 1 + extra_len, 0).astype(jnp.int32)
    later_sum = jnp.sum(member * later_len[:, None], axis=0).astype(jnp.int32)
    ceiling = CAP - later_sum
    leading = jax.random.randint(sub_keys[4], (N_DP,), CAP // 2 + 1, ceiling + 1, dtype=jnp.int32)
    leading = jnp.where(jnp.arange(N_DP, dtype=jnp.int32) == full_group, ceiling, leading)
    lead_of = jnp.sum(member * leading[None, :], axis=1).astype(jnp.int32)
    lengths = jnp.where(rank_in == 0, lead_of, later_len).astype(jnp.int32)
    return (lengths, groups)


def draw_seq_lens(key, part):
    plan = sequence_plan(key)
    return plan[0]


def draw_seq_groups(key, part):
    plan = sequence_plan(key)
    return plan[1]


def levels(key, dims, cuts, smallest, high):
    def one(dim, parts):
        draws = jax.random.uniform(jax.random.fold_in(jax.random.fold_in(key, 6), dim), (parts,), jnp.float32, smallest / len(cuts), high / len(cuts))
        return jnp.repeat(jnp.exp(draws), dims[dim] // parts).reshape((-1,) + (1,) * (len(dims) - dim - 1))

    factor_of = one(*cuts[0])
    for cut in cuts[1:]:
        factor_of = factor_of * one(*cut)
    return factor_of


def gaussian(own_key, dims, width, most, shards=(), kind=jnp.bfloat16):
    values = jax.random.normal(own_key, dims, jnp.float32) * width
    if len(shards) > 0:
        values = levels(own_key, dims, shards, -0.22, 0.18) * values
    return jnp.clip(values, min=-most, max=most).astype(kind)


def setup_inputs(seed: int = 0) -> dict:
    arg_keys = jax.random.split(jax.random.key(seed), 18)
    x_in = gaussian(arg_keys[0], (TOKENS, D), 1.0, 6.0, ((0, 8), (1, 4)))
    seq_lens = draw_seq_lens(jax.random.fold_in(arg_keys[17], 71), 0)
    seq_groups = draw_seq_groups(jax.random.fold_in(arg_keys[17], 71), 0)
    ln1_gain = jnp.clip(1.0 + 0.1 * jax.random.normal(arg_keys[3], (D,), jnp.float32), 0.5, 1.5)
    ln1_bias = gaussian(arg_keys[4], (D,), 0.3, 1.5, ((0, 4),), jnp.float32)
    w_query = gaussian(arg_keys[5], (QK, D), D ** -0.5, 0.125, ((0, 2), (1, 4)))
    w_key = gaussian(arg_keys[6], (QK, D), D ** -0.5, 0.125, ((0, 2), (1, 4)))
    w_value = gaussian(arg_keys[7], (VDIM, D), D ** -0.5, 0.125, ((0, 2), (1, 4)))
    w_swish = gaussian(arg_keys[8], (VDIM, D), D ** -0.5, 0.125, ((0, 2), (1, 4)))
    gn_gain = jnp.clip(1.0 + 0.1 * jax.random.normal(arg_keys[9], (VDIM,), jnp.float32), 0.5, 1.5)
    w_out = gaussian(arg_keys[10], (D, VDIM), VDIM ** -0.5, 0.09375, ((0, 4), (1, 2)))
    ln2_gain = jnp.clip(1.0 + 0.1 * jax.random.normal(arg_keys[11], (D,), jnp.float32), 0.5, 1.5)
    ln2_bias = gaussian(arg_keys[12], (D,), 0.3, 1.5, ((0, 4),), jnp.float32)
    w_mlp_gate = gaussian(arg_keys[13], (FF, D), D ** -0.5, 0.125, ((0, 2), (1, 4)))
    w_mlp_up = gaussian(arg_keys[14], (FF, D), D ** -0.5, 0.125, ((0, 2), (1, 4)))
    w_down = gaussian(arg_keys[15], (D, FF), FF ** -0.5, 0.09375, ((0, 4), (1, 2)))
    d_out = gaussian(arg_keys[16], (TOKENS, D), 1.0, 6.0, ((0, 8), (1, 4)))
    return {"x_in": x_in, "seq_lens": seq_lens, "seq_groups": seq_groups, "ln1_gain": ln1_gain, "ln1_bias": ln1_bias, "w_query": w_query, "w_key": w_key, "w_value": w_value, "w_swish": w_swish, "gn_gain": gn_gain, "w_out": w_out, "ln2_gain": ln2_gain, "ln2_bias": ln2_bias, "w_mlp_gate": w_mlp_gate, "w_mlp_up": w_mlp_up, "w_down": w_down, "d_out": d_out}


@jax.custom_vjp
def low(v):
    return lax.optimization_barrier(v.astype(jnp.bfloat16)).astype(jnp.float32)

@jax.custom_vjp
def low_back(v):
    return v

def low_keep(v):
    return (low(v), None)

def low_pass(kept, grad):
    return (grad,)

def back_keep(v):
    return (v, None)

def back_low(kept, grad):
    return (low(grad),)
low.defvjp(low_keep, low_pass)
low_back.defvjp(back_keep, back_low)
NORM_EPS = 1e-05
GROUP_EPS = 1.0

def slot_layout(seq_lens, seq_groups, group_index, slot_count):
    is_mine = seq_groups == group_index
    own_lengths = jnp.where(is_mine, seq_lens, 0).astype(jnp.int32)
    starts = (jnp.cumsum(own_lengths) - own_lengths).astype(jnp.int32)
    slot_ids = jnp.arange(slot_count, dtype=jnp.int32)
    inside = is_mine[None, :] & (slot_ids[:, None] >= starts[None, :]) & (slot_ids[:, None] < (starts + own_lengths)[None, :])
    is_valid = jnp.any(inside, axis=1)
    number = jnp.arange(seq_lens.shape[0], dtype=jnp.int32)
    found = lax.optimization_barrier(jnp.sum(jnp.where(inside, number[None, :], 0), axis=1)).astype(jnp.int32)
    segment = jnp.where(is_valid, found, -1).astype(jnp.int32)
    offsets = lax.optimization_barrier(jnp.sum(jnp.where(inside, starts[None, :], 0), axis=1)).astype(jnp.int32)
    position = (slot_ids - offsets).astype(jnp.float32)
    return (segment, position)

def rotate_scale(values, position, direction):
    half_width = values.shape[-1] // 2
    pair_index = jnp.arange(half_width, dtype=jnp.float32)
    frequency = jnp.exp(pair_index * (-math.log(10000.0) / half_width))
    zeta_base = (pair_index / half_width + 0.4) / 1.4
    angles = position[:, None] * frequency[None, :]
    growth = jnp.exp(direction / 512.0 * position[:, None] * jnp.log(zeta_base)[None, :])
    cos_scaled = jnp.cos(angles) * growth
    sin_scaled = jnp.sin(angles) * growth
    first_half = values[:, :half_width]
    second_half = values[:, half_width:]
    return jnp.concatenate([first_half * cos_scaled - second_half * sin_scaled, second_half * cos_scaled + first_half * sin_scaled], axis=1)

def decay_block(row_segment, all_segment, row_slots, all_slots, log_rate):
    distance = row_slots[:, None] - all_slots[None, :]
    allowed = (row_segment[:, None] == all_segment[None, :]) & (row_segment[:, None] >= 0) & (distance >= 0)
    steps_back = jnp.maximum(distance, 0).astype(jnp.float32)
    return jnp.where(allowed, jnp.exp(steps_back * log_rate), 0.0)

def head_mix(retained, gate_raw, gain_vec):
    average = lax.optimization_barrier(jnp.mean(retained, axis=1, keepdims=True))
    centered = retained - average
    variance = lax.optimization_barrier(jnp.mean(centered * centered, axis=1, keepdims=True))
    normed = centered * lax.rsqrt(variance + GROUP_EPS) * gain_vec
    return jax.nn.silu(gate_raw) * normed

def gelu_mix(gate_raw, up_raw):
    return jax.nn.gelu(gate_raw, approximate=True) * up_raw

def layer_norm(values, gain_vec, bias_vec):
    average = lax.optimization_barrier(jnp.mean(values, axis=1, keepdims=True))
    centered = values - average
    variance = lax.optimization_barrier(jnp.mean(centered * centered, axis=1, keepdims=True))
    return centered * lax.rsqrt(variance + NORM_EPS) * gain_vec + bias_vec

def project(left, weight):
    return lax.dot_general(left, weight, (((1,), (1,)), ((), ())), precision=lax.Precision.HIGHEST, preferred_element_type=jnp.float32)

def retain_head(operands, segment, position):
    query_raw, key_raw, value_low, gate_raw, gain_vec, log_rate = operands
    query = low(rotate_scale(query_raw, position, 1.0))
    key_rot = low(rotate_scale(key_raw, position, -1.0))
    slot_ids = jnp.arange(segment.shape[0], dtype=jnp.int32)
    decay = decay_block(segment, segment, slot_ids, slot_ids, log_rate)
    scores = low_back(jnp.dot(query, key_rot.T, precision=lax.Precision.HIGHEST, preferred_element_type=jnp.float32))
    weights = low(scores * (1.0 / math.sqrt(query.shape[1])) * decay)
    retained = low_back(jnp.dot(weights, value_low, precision=lax.Precision.HIGHEST, preferred_element_type=jnp.float32))
    return low(head_mix(retained, gate_raw, gain_vec))

def group_forward(params, x_group, segment, position):
    ln1_gain, ln1_bias, w_query, w_key, w_value, w_swish, gn_gain, w_out, ln2_gain, ln2_bias, w_mlp_gate, w_mlp_up, w_down = params
    normed1 = low(layer_norm(x_group, ln1_gain, ln1_bias))
    query_raw = low_back(project(normed1, w_query))
    key_raw = low_back(project(normed1, w_key))
    value_low = low(low_back(project(normed1, w_value)))
    swish_raw = low_back(project(normed1, w_swish))
    log_rates = jnp.log1p(-jnp.exp2(-5.0 - jnp.arange(HEADS, dtype=jnp.float32)))

    def per_head(operands):
        return jax.checkpoint(retain_head)(operands, segment, position)
    heads_low = lax.map(per_head, (query_raw.reshape(CAP, HEADS, KD).transpose(1, 0, 2), key_raw.reshape(CAP, HEADS, KD).transpose(1, 0, 2), value_low.reshape(CAP, HEADS, VH).transpose(1, 0, 2), swish_raw.reshape(CAP, HEADS, VH).transpose(1, 0, 2), gn_gain.reshape(HEADS, VH), log_rates))
    heads_low = heads_low.transpose(1, 0, 2).reshape(CAP, VDIM)
    resid = x_group + low_back(project(heads_low, w_out))
    normed2 = low(layer_norm(resid, ln2_gain, ln2_bias))
    gate_raw = low_back(project(normed2, w_mlp_gate))
    up_raw = low_back(project(normed2, w_mlp_up))
    hidden_low = low(gelu_mix(gate_raw, up_raw))
    return resid + low_back(project(hidden_low, w_down))

def reference(x_in, seq_lens, seq_groups, ln1_gain, ln1_bias, w_query, w_key, w_value, w_swish, gn_gain, w_out, ln2_gain, ln2_bias, w_mlp_gate, w_mlp_up, w_down, d_out):
    params = tuple((item.astype(jnp.float32) for item in (ln1_gain, ln1_bias, w_query, w_key, w_value, w_swish, gn_gain, w_out, ln2_gain, ln2_bias, w_mlp_gate, w_mlp_up, w_down)))
    group_ids = jnp.arange(N_DP, dtype=jnp.int32)
    segments, positions = jax.vmap(lambda group_index: slot_layout(seq_lens, seq_groups, group_index, CAP))(group_ids)
    x_groups = x_in.astype(jnp.float32).reshape(N_DP, CAP, D)
    cotangent = d_out.astype(jnp.float32).reshape(N_DP, CAP, D) * (segments >= 0).astype(jnp.float32)[:, :, None]

    def forward(weights, inputs):

        def step_group(totals, operands):
            x_group, segment, position = operands
            return (totals, jax.checkpoint(group_forward)(weights, x_group, segment, position))
        _, outputs = lax.scan(step_group, jnp.zeros((), jnp.float32), (inputs, segments, positions))
        return outputs
    y_groups, pull_back = jax.vjp(forward, params, x_groups)
    d_params, d_groups = pull_back(cotangent)
    return (y_groups.reshape(N_DP * CAP, D), d_groups.reshape(N_DP * CAP, D), d_params[0], d_params[1], d_params[2], d_params[3], d_params[4], d_params[5], d_params[6], d_params[7], d_params[8], d_params[9], d_params[10], d_params[11], d_params[12])
```

```python
import functools
import itertools
import math

import jax
import jax.numpy as jnp
from jax import lax
from jax.sharding import PartitionSpec as P

NORM_EPS = 1e-05
GROUP_EPS = 1.0
AXES = ("dp", "row", "col")
BF16 = jnp.bfloat16
F32 = jnp.float32


def permute(value, change, reps):
    pairs = []
    for r, c, x, zh, zl in itertools.product(range(reps), range(2), range(2), range(2), range(2)):
        r2, c2, x2, zh2, zl2 = change(r, c, x, zh, zl)
        source = ((2 * r + c) * 2 + x) * 4 + 2 * zh + zl
        target = ((2 * r2 + c2) * 2 + x2) * 4 + 2 * zh2 + zl2
        pairs.append((source, target))
    return lax.ppermute(value, AXES, pairs)


class Links:
    def __init__(self, reps):
        self.reps = reps

    def x(self, value):
        return permute(value, lambda r, c, x, zh, zl: (r, c, 1 - x, zh, zl), self.reps)

    def z(self, value):
        return permute(value, lambda r, c, x, zh, zl: (r, c, x, zh, 1 - zl), self.reps)

    def c(self, value):
        return permute(value, lambda r, c, x, zh, zl: (r, 1 - c, x, zh, zl), self.reps)

    def swap(self, value):
        return permute(value, lambda r, c, x, zh, zl: (r, zh, x, c, zl), self.reps)

    def col(self, value, k):
        return permute(
            value, lambda r, c, x, zh, zl: (r, c, x, zh ^ (k >> 1), zl ^ (k & 1)), self.reps
        )

    def r(self, value, k):
        return permute(
            value, lambda r, c, x, zh, zl: ((r + k) % self.reps, c, x, zh, zl), self.reps
        )

    def home(self, value, k):
        def change(r, c, x, zh, zl):
            target = (2 * c + zl) ^ k
            return (r, zh, x, target >> 1, target & 1)

        return permute(value, change, self.reps)


def slot_layout(seq_lens, seq_groups, group_index, slot_ids):
    is_mine = seq_groups == group_index
    own_lengths = jnp.where(is_mine, seq_lens, 0)
    starts = jnp.cumsum(own_lengths) - own_lengths
    inside = (
        is_mine[None, :]
        & (slot_ids[:, None] >= starts[None, :])
        & (slot_ids[:, None] < (starts + own_lengths)[None, :])
    )
    is_valid = jnp.any(inside, axis=1)
    number = jnp.arange(seq_lens.shape[0], dtype=jnp.int32)
    found = jnp.sum(jnp.where(inside, number[None, :], 0), axis=1)
    segment = jnp.where(is_valid, found, -1)
    offsets = jnp.sum(jnp.where(inside, starts[None, :], 0), axis=1)
    position = (slot_ids - offsets).astype(F32)
    return (segment, position)


def rotate_scale(values, position, direction):
    half_width = values.shape[-1] // 2
    pair_index = jnp.arange(half_width, dtype=F32)
    frequency = jnp.exp(pair_index * (-math.log(10000.0) / half_width))
    zeta_base = (pair_index / half_width + 0.4) / 1.4
    angles = position[:, None] * frequency[None, :]
    growth = jnp.exp(direction / 512.0 * position[:, None] * jnp.log(zeta_base)[None, :])
    cos_scaled = jnp.cos(angles) * growth
    sin_scaled = jnp.sin(angles) * growth
    first_half = values[:, :half_width]
    second_half = values[:, half_width:]
    return jnp.concatenate(
        [
            first_half * cos_scaled - second_half * sin_scaled,
            second_half * cos_scaled + first_half * sin_scaled,
        ],
        axis=1,
    )


def head_mix(retained, gate_raw, gain_vec):
    average = jnp.mean(retained, axis=1, keepdims=True)
    centered = retained - average
    variance = jnp.mean(centered * centered, axis=1, keepdims=True)
    normed = centered * lax.rsqrt(variance + GROUP_EPS) * gain_vec
    return jax.nn.silu(gate_raw) * normed


def gelu_mix(gate_raw, up_raw):
    return jax.nn.gelu(gate_raw, approximate=True) * up_raw


def contract_last(left, right):
    return lax.dot_general(left, right, (((1,), (1,)), ((), ())), preferred_element_type=F32)


def contract_first(left, right):
    return lax.dot_general(left, right, (((0,), (0,)), ((), ())), preferred_element_type=F32)


def dot(left, right):
    return jnp.dot(left, right, preferred_element_type=F32)


def center(values):
    average = jnp.mean(values, axis=1, keepdims=True)
    shifted = values - average
    inverse = lax.rsqrt(jnp.mean(shifted * shifted, axis=1, keepdims=True) + NORM_EPS)
    return (shifted * inverse, inverse)


def norm_backward(d_normed, centered, inverse, gain_vec):
    d_gain = jnp.sum(d_normed * centered, axis=0)
    d_bias = jnp.sum(d_normed, axis=0)
    d_scaled = d_normed * gain_vec
    mean_first = jnp.mean(d_scaled, axis=1, keepdims=True)
    mean_cross = jnp.mean(d_scaled * centered, axis=1, keepdims=True)
    return (inverse * (d_scaled - mean_first - centered * mean_cross), d_gain, d_bias)


def scaled_decay(segment, slots, log_rate, width):
    distance = slots[:, None] - slots[None, :]
    allowed = (
        (segment[:, None] == segment[None, :]) & (segment[:, None] >= 0) & (distance >= 0)
    )
    steps_back = jnp.maximum(distance, 0).astype(F32)
    return jnp.where(allowed, jnp.exp(steps_back * log_rate), 0.0) / math.sqrt(width)


def gather_rows(own, links):
    rows, width = own.shape
    half = width // 2
    first, second = (own[:, :half], own[:, half:])
    first_z = links.z(first)
    second_x = links.x(second)
    first_pair = jnp.stack([first, first_z])
    second_pair = jnp.stack([second, second_x])
    first_x = links.x(first_pair)
    second_z = links.z(second_pair)
    first_all = jnp.stack([first_pair, first_x])
    second_all = jnp.stack([second_pair, second_z], axis=1)
    mine = jnp.concatenate([first_all, second_all], axis=-1)
    other = links.c(mine)
    return jnp.stack([mine, other], axis=1).reshape(8 * rows, width)


def scatter_rows(half_of, links, width):
    arriving = links.c(half_of(1))
    chip_sum = half_of(0).astype(F32) + arriving.astype(F32)
    half = width // 2
    first, second = (chip_sum[..., :half], chip_sum[..., half:])
    first = first[0] + links.x(first[1].astype(BF16)).astype(F32)
    second = second[:, 0] + links.z(second[:, 1].astype(BF16)).astype(F32)
    first = first[0] + links.z(first[1].astype(BF16)).astype(F32)
    second = second[0] + links.x(second[1].astype(BF16)).astype(F32)
    return jnp.concatenate([first, second], axis=-1)


def half_rows(value, jc):
    rows = value.shape[0] // 8
    return value.reshape(2, 2, 2 * rows, -1)[:, jc].reshape(4 * rows, -1)


def partial_product(left, weight, links, transposed):
    width = weight.shape[0] if transposed else weight.shape[1]
    rows = left.shape[0] // 8

    def half_of(jc):
        part = half_rows(left, jc)
        product = contract_last(part, weight) if transposed else dot(part, weight)
        return product.astype(BF16).reshape(2, 2, rows, width)

    return scatter_rows(half_of, links, width)


def gather_block(block, links, c, zl):
    block_rows, block_width = block.shape
    half = block_rows // 2
    first, second = (block[:half], block[half:])
    first_z = links.z(first)
    second_x = links.x(second)
    first_pair = jnp.stack([first, first_z])
    second_pair = jnp.stack([second, second_x])
    first_x = links.x(first_pair)
    second_z = links.z(second_pair)
    first_all = jnp.stack([first_pair, first_x])
    second_all = jnp.stack([second_pair, second_z], axis=1)
    mine = jnp.concatenate([first_all, second_all], axis=2)
    other = links.c(mine)
    both = jnp.stack([mine, other])
    columns = []
    for fc, fz in itertools.product(range(2), range(2)):
        piece = lax.dynamic_index_in_dim(both, c ^ fc, 0, keepdims=False)
        columns.append(lax.dynamic_index_in_dim(piece, zl ^ fz, 1, keepdims=False))
    whole = jnp.concatenate(columns, axis=-1)
    whole = whole.reshape(2, 4, block_rows // 4, -1)
    own = 2 * c + zl
    blocks = [lax.dynamic_index_in_dim(whole, own ^ j, 1, keepdims=True) for j in range(4)]
    return jnp.concatenate(blocks, axis=1).reshape(2 * block_rows, -1)


def send_home(own, links, c, zl, z):
    rows, width = own.shape
    part = width // 4
    low = own.astype(BF16)
    out = jnp.zeros((4 * rows, part), F32)
    for k in range(4):
        piece = lax.dynamic_slice_in_dim(low, ((2 * c + zl) ^ k) * part, part, 1)
        got = links.home(piece, k).astype(F32)
        out = lax.dynamic_update_slice_in_dim(out, got, (z ^ k) * rows, 0)
    return out


def head_rows(weight, head):
    size = weight.shape[0] // 4
    return lax.dynamic_slice_in_dim(weight, head * size, size, 0)


def head_columns(weight, head):
    size = weight.shape[1] // 4
    return lax.dynamic_slice_in_dim(weight, head * size, size, 1)


def fetch_rows(weights, links, c, r, z):
    reps = links.reps
    width = weights[0].shape[1]
    part = width // reps

    def stacked(k):
        head = ((z ^ k) & 1) * 2 + c
        return jnp.concatenate([head_rows(weight, head) for weight in weights], axis=0)

    own = stacked(0)
    out = jnp.zeros((own.shape[0], 4 * width), BF16)
    out = lax.dynamic_update_slice_in_dim(out, own, z * width, 1)
    for k in (2, 3, 1):
        piece = lax.dynamic_slice_in_dim(stacked(k), r * part, part, 1)
        got = links.col(piece, k)
        out = lax.dynamic_update_slice_in_dim(out, got, (z ^ k) * width + r * part, 1)
        for step in range(1, reps):
            more = links.r(got, step)
            place = (z ^ k) * width + ((r - step) % reps) * part
            out = lax.dynamic_update_slice_in_dim(out, more, place, 1)
    return out


def fetch_columns(weight, links, c, r, z):
    reps = links.reps
    height = weight.shape[0]
    part = height // reps
    own = head_columns(weight, (z & 1) * 2 + c)
    out = jnp.zeros((4 * height, own.shape[1]), BF16)
    out = lax.dynamic_update_slice_in_dim(out, own, z * height, 0)
    for k in (2, 3, 1):
        rows = lax.dynamic_slice_in_dim(weight, r * part, part, 0)
        got = links.col(head_columns(rows, ((z ^ k) & 1) * 2 + c), k)
        out = lax.dynamic_update_slice_in_dim(out, got, (z ^ k) * height + r * part, 0)
        for step in range(1, reps):
            more = links.r(got, step)
            place = (z ^ k) * height + ((r - step) % reps) * part
            out = lax.dynamic_update_slice_in_dim(out, more, place, 0)
    return out


def reduce_grad(pieces, links, c, r, z):
    reps = links.reps
    total = lax.dynamic_index_in_dim(pieces, r, 0, keepdims=False).astype(F32)
    for step in range(1, reps):
        outgoing = lax.dynamic_index_in_dim(pieces, (r + step) % reps, 0, keepdims=False)
        total = total + links.r(outgoing, step).astype(F32)
    low = total.astype(BF16)

    def block(k):
        return lax.dynamic_index_in_dim(low, z ^ k, 0, keepdims=False)

    arrived = [block(0)] + [links.col(block(k), k) for k in (1, 2, 3)]
    same = (arrived[0].astype(F32) + arrived[2].astype(F32)).astype(BF16)
    crossed = (arrived[1].astype(F32) + arrived[3].astype(F32)).astype(BF16)
    is_low = (z & 1) == 0
    heads = jnp.stack([jnp.where(is_low, same, crossed), jnp.where(is_low, crossed, same)])
    gathered = jnp.zeros((reps,) + heads.shape, BF16)
    gathered = lax.dynamic_update_index_in_dim(gathered, heads, r, 0)
    for step in range(1, reps):
        more = links.r(heads, step)
        gathered = lax.dynamic_update_index_in_dim(gathered, more, (r - step) % reps, 0)
    other = links.c(gathered)
    first = jnp.where(c == 0, gathered, other)
    second = jnp.where(c == 0, other, gathered)
    both = jnp.stack([first, second])
    return both


def row_grads(grad, counts, links, c, r, z):
    reps = links.reps
    outs, inputs = grad.shape
    part = inputs // 4 // reps
    pieces = grad.astype(BF16).reshape(outs, 4, reps, part).transpose(2, 1, 0, 3)
    both = reduce_grad(pieces, links, c, r, z)
    ordered = both.transpose(2, 0, 3, 1, 4).reshape(4, outs, inputs // 4)
    results = []
    offset = 0
    for count in counts:
        piece = ordered[:, offset : offset + count]
        results.append(piece.reshape(4 * count, inputs // 4).astype(F32))
        offset += count
    return results


def column_grad(grad, links, c, r, z):
    reps = links.reps
    outs, inputs = grad.shape
    part = outs // 4 // reps
    pieces = grad.astype(BF16).reshape(4, reps, part, inputs).transpose(1, 0, 2, 3)
    both = reduce_grad(pieces, links, c, r, z)
    return both.transpose(1, 3, 2, 0, 4).reshape(outs // 4, 4 * inputs).astype(F32)


def body(
    x_in,
    seq_lens,
    seq_groups,
    ln1_gain,
    ln1_bias,
    w_query,
    w_key,
    w_value,
    w_swish,
    gn_gain,
    w_out,
    ln2_gain,
    ln2_bias,
    w_mlp_gate,
    w_mlp_up,
    w_down,
    d_out,
):
    reps = lax.axis_size("dp") // 2
    links = Links(reps)
    dp_at = lax.axis_index("dp")
    r, c = (dp_at // 2, dp_at % 2)
    x = lax.axis_index("row")
    z = lax.axis_index("col")
    zh, zl = (z // 2, z % 2)
    block_rows, block_width = x_in.shape
    rows = block_rows // 4
    width = block_width * 4
    key_width = w_query.shape[0] // 4
    value_width = w_value.shape[0] // 4
    ffn_width = w_mlp_gate.shape[0] // 4
    head_at = 2 * zl + c

    vectors = jnp.stack([ln1_gain, ln1_bias, ln2_gain, ln2_bias, gn_gain])
    vectors = lax.all_gather(vectors, "col", axis=1, tiled=True)
    gain1, bias1, gain2, bias2 = (vectors[i] for i in range(4))
    gain_vec = lax.dynamic_slice_in_dim(vectors[4], head_at * value_width, value_width, 0)

    blocks = jnp.arange(8, dtype=jnp.int32)
    natural = (x ^ (blocks >> 2)) * 4 + (c ^ ((blocks >> 1) & 1)) * 2 + (zl ^ (blocks & 1))
    slots = (natural[:, None] * rows + jnp.arange(rows, dtype=jnp.int32)[None, :]).reshape(-1)
    segment, position = slot_layout(seq_lens, seq_groups, 2 * r + zh, slots)
    keep_rows = (segment >= 0)[:, None]
    log_rate = jnp.log1p(-jnp.exp2(-5.0 - (4 * x + head_at).astype(F32)))
    decay = scaled_decay(segment, slots, log_rate, key_width)

    x_all = gather_block(links.swap(x_in), links, c, zl)
    weight_in = fetch_rows((w_query, w_key, w_value, w_swish), links, c, r, z)
    x_own = x_all[:rows].astype(F32)
    normed1 = (center(x_all.astype(F32))[0] * gain1 + bias1).astype(BF16)
    projected = contract_last(normed1, weight_in)
    query_raw = projected[:, :key_width]
    key_raw = projected[:, key_width : 2 * key_width]
    value_low = projected[:, 2 * key_width : 2 * key_width + value_width].astype(BF16)
    swish_raw = projected[:, 2 * key_width + value_width :]
    query_rot, query_pull = jax.vjp(
        functools.partial(rotate_scale, position=position, direction=1.0), query_raw
    )
    key_rot, key_pull = jax.vjp(
        functools.partial(rotate_scale, position=position, direction=-1.0), key_raw
    )
    query_low = query_rot.astype(BF16)
    key_low = key_rot.astype(BF16)
    weights = (contract_last(query_low, key_low) * decay).astype(BF16)
    retained = dot(weights, value_low)
    mixed_heads, mix_pull = jax.vjp(head_mix, retained, swish_raw, gain_vec)
    heads_low = mixed_heads.astype(BF16)
    weight_out = fetch_columns(w_out, links, c, r, z)
    attn_own = partial_product(heads_low, weight_out, links, True)
    weight_ffn = fetch_rows((w_mlp_gate, w_mlp_up), links, c, r, z)
    resid = x_own + attn_own
    centered2, inverse2 = center(resid)
    normed2 = gather_rows((centered2 * gain2 + bias2).astype(BF16), links)
    gate_up = contract_last(normed2, weight_ffn)
    hidden_value, hidden_pull = jax.vjp(gelu_mix, gate_up[:, :ffn_width], gate_up[:, ffn_width:])
    hidden_low = hidden_value.astype(BF16)
    weight_down = fetch_columns(w_down, links, c, r, z)

    grad_all = gather_block(links.swap(d_out), links, c, zl)
    grad_all = jnp.where(keep_rows, grad_all, 0)
    grad_own = grad_all[:rows].astype(F32)
    d_hidden = dot(grad_all, weight_down)
    d_gate, d_up = hidden_pull(d_hidden)
    grad_ffn = jnp.concatenate([d_gate, d_up], axis=1).astype(BF16)
    d_normed2 = partial_product(grad_ffn, weight_ffn, links, False)
    d_w_down = column_grad(contract_first(grad_all, hidden_low), links, c, r, z)
    ffn_own = partial_product(hidden_low, weight_down, links, True)
    y_out = send_home(resid + ffn_own, links, c, zl, z)
    d_w_mlp_gate, d_w_mlp_up = row_grads(
        contract_first(grad_ffn, normed2), (ffn_width, ffn_width), links, c, r, z
    )
    d_resid_part, d_ln2_gain, d_ln2_bias = norm_backward(d_normed2, centered2, inverse2, gain2)
    d_resid = grad_own + d_resid_part
    d_resid_all = gather_rows(d_resid.astype(BF16), links)
    d_heads = dot(d_resid_all, weight_out)
    d_w_out = column_grad(contract_first(d_resid_all, heads_low), links, c, r, z)
    d_retained, d_swish, d_gn_gain = mix_pull(d_heads)
    d_retained = d_retained.astype(BF16)
    d_scores = (contract_last(d_retained, value_low) * decay).astype(BF16)
    d_query = dot(d_scores, key_low)
    d_key = contract_first(d_scores, query_low)
    d_value = contract_first(weights, d_retained)
    (d_query_raw,) = query_pull(d_query)
    (d_key_raw,) = key_pull(d_key)
    grad_attn = jnp.concatenate([d_query_raw, d_key_raw, d_value, d_swish], axis=1).astype(BF16)
    d_normed1 = partial_product(grad_attn, weight_in, links, False)
    (d_w_swish,) = row_grads(
        contract_first(grad_attn[:, 2 * key_width + value_width :], normed1),
        (value_width,), links, c, r, z,
    )
    d_w_query, d_w_key, d_w_value = row_grads(
        contract_first(grad_attn[:, : 2 * key_width + value_width], normed1),
        (key_width, key_width, value_width), links, c, r, z,
    )
    centered1, inverse1 = center(x_own)
    d_input_part, d_ln1_gain, d_ln1_bias = norm_backward(d_normed1, centered1, inverse1, gain1)
    d_x_in = send_home(d_resid + d_input_part, links, c, zl, z)

    gn_places = jnp.zeros((2, 4, value_width), F32)
    gn_places = lax.dynamic_update_slice(gn_places, d_gn_gain[None, None], (x, head_at, 0))
    summed = lax.psum(
        jnp.concatenate(
            [d_ln1_gain, d_ln1_bias, d_ln2_gain, d_ln2_bias, gn_places.reshape(-1)]
        ).reshape(-1, width),
        AXES,
    )
    mine = lax.dynamic_slice_in_dim(summed[:4], z * block_width, block_width, 1)
    d_gn_gain = lax.dynamic_slice(
        summed[4:].reshape(8, value_width), (4 * x + z, 0), (1, value_width)
    ).reshape(-1)
    return (
        y_out,
        d_x_in,
        mine[0],
        mine[1],
        d_w_query,
        d_w_key,
        d_w_value,
        d_w_swish,
        d_gn_gain,
        d_w_out,
        mine[2],
        mine[3],
        d_w_mlp_gate,
        d_w_mlp_up,
        d_w_down,
    )


def solution(mesh):
    return jax.shard_map(
        body,
        mesh=mesh,
        in_specs=(
            P(("dp", "row"), "col"),
            P(),
            P(),
            P("col"),
            P("col"),
            P("row", "col"),
            P("row", "col"),
            P("row", "col"),
            P("row", "col"),
            P(("row", "col")),
            P("col", "row"),
            P("col"),
            P("col"),
            P("row", "col"),
            P("row", "col"),
            P("col", "row"),
            P(("dp", "row"), "col"),
        ),
        out_specs=(
            P(("dp", "row"), "col"),
            P(("dp", "row"), "col"),
            P("col"),
            P("col"),
            P("row", "col"),
            P("row", "col"),
            P("row", "col"),
            P("row", "col"),
            P(("row", "col")),
            P("col", "row"),
            P("col"),
            P("col"),
            P("row", "col"),
            P("row", "col"),
            P("col", "row"),
        ),
        check_vma=False,
    )
```

```python
import functools, itertools, math
import jax, jax.numpy as jnp
from jax import lax
from jax.experimental import pallas as pl
from jax.experimental.pallas import tpu as pltpu
from jax.sharding import PartitionSpec as P
BF16=jnp.bfloat16; F32=jnp.float32; MESH=pl.DeviceIdType.MESH
NORM_EPS=1e-5; GROUP_EPS=1.0
AXES=("dp","row","col")

def dot_nt(a,b): return lax.dot_general(a,b,(((1,),(1,)),((),())),preferred_element_type=F32)
def dot_nn(a,b): return lax.dot_general(a,b,(((1,),(0,)),((),())),preferred_element_type=F32)
def dot_tn(a,b): return lax.dot_general(a,b,(((0,),(0,)),((),())),preferred_element_type=F32)

class Net:
    def __init__(self, reps, send, recv, local):
        self.reps=reps; self.send=send; self.recv=recv; self.local_sems=local
        self.used=0; self.used_local=0; self.sent=[]
        dp=lax.axis_index("dp")
        self.r=dp//2; self.c=dp%2
        self.x=lax.axis_index("row")
        self.z=lax.axis_index("col")
        self.zh=self.z//2; self.zl=self.z%2
    def flip(self, v): return 1-v
    def xor(self, k):
        zh = 1-self.zh if k & 2 else self.zh
        zl = 1-self.zl if k & 1 else self.zl
        return 2*zh+zl
    def at(self, r=None, c=None, x=None, z=None):
        r=self.r if r is None else r; c=self.c if c is None else c
        x=self.x if x is None else x; z=self.z if z is None else z
        return {"dp":2*r+c,"row":x,"col":z}
    def to_x(self): return self.at(x=1-self.x)
    def to_z(self): return self.at(z=self.xor(1))
    def to_c(self): return self.at(c=1-self.c)
    def to_col(self,k): return self.at(z=self.xor(k))
    def to_r(self,s): return self.at(r=lax.rem(self.r+s,self.reps))
    def from_r(self,s): return lax.rem(self.r+self.reps-s,self.reps)
    def copy(self, src, dst, device, start=True):
        i=self.used; self.used+=1
        assert i<self.send.shape[0], "more semaphores"
        h=pltpu.make_async_remote_copy(src,dst,self.send.at[i],self.recv.at[i],device_id=device,device_id_type=MESH)
        if start: h.start(); self.sent.append(h)
        return h
    def move(self, src, dst):
        i=self.used_local; self.used_local+=1
        assert i<self.local_sems.shape[0], "more semaphores"
        h=pltpu.make_async_copy(src,dst,self.local_sems.at[i]); h.start(); return h
    def barrier(self):
        sem=pltpu.get_barrier_semaphore()
        n=0
        for c,zh,zl in itertools.product(range(2),range(2),range(2)):
            if (c,zh,zl)==(0,0,0): continue
            cc=1-self.c if c else self.c
            z=2*(1-self.zh if zh else self.zh)+(1-self.zl if zl else self.zl)
            pl.semaphore_signal(sem,inc=1,device_id=self.at(c=cc,z=z),device_id_type=MESH); n+=1
        pl.semaphore_signal(sem,inc=1,device_id=self.to_x(),device_id_type=MESH); n+=1
        for s in range(1,self.reps):
            pl.semaphore_signal(sem,inc=1,device_id=self.to_r(s),device_id_type=MESH); n+=1
        pl.semaphore_wait(sem,n)
    def finish(self):
        for h in self.sent: h.wait_send()
        self.sent=[]

class Gather:
    def __init__(self, net, view):
        self.net=net; self.view=view
    def block(self, jx, jc, jz, half=None):
        n=self.net
        return self.view(1-n.x if jx else n.x, 1-n.c if jc else n.c, 1-n.zl if jz else n.zl, half)
    def send(self, jx,jc,jz,half,device):
        b=self.block(jx,jc,jz,half); return self.net.copy(b,b,device)
    def start(self):
        n=self.net
        self.fx=self.send(0,0,0,None,n.to_x())
        self.fz=self.send(0,0,0,None,n.to_z())
        self.fc=self.send(0,0,0,None,n.to_c())
    def after_z(self):
        n=self.net
        self.fz.wait_recv()
        self.dx=self.send(0,0,1,0,n.to_x())
        self.cz=self.send(0,0,1,None,n.to_c())
    def after_x(self):
        n=self.net
        self.fx.wait_recv()
        self.dz=self.send(1,0,0,1,n.to_z())
        self.cx=self.send(1,0,0,None,n.to_c())
    def after_diag(self):
        n=self.net
        self.dx.wait_recv(); self.c0=self.send(1,0,1,0,n.to_c())
        self.dz.wait_recv(); self.c1=self.send(1,0,1,1,n.to_c())
    def wait_c(self):
        for h in (self.fc,self.cz,self.cx,self.c0,self.c1): h.wait_recv()

class Fetch:
    def __init__(self, net, src, dst, offset, size, by_columns):
        self.net=net; self.src=src; self.dst=dst; self.offset=offset; self.size=size; self.by_columns=by_columns
        self.part=size//net.reps
    def source(self, head, first, count):
        if self.by_columns:
            w=self.src.shape[1]//4
            return self.src.at[pl.ds(first,count), pl.ds(pl.multiple_of(head*w,w),w)]
        return self.src.at[pl.ds(pl.multiple_of(head*self.size+first,16),count),:]
    def place(self, z, r):
        return self.dst.at[z, pl.ds(pl.multiple_of(self.offset+r*self.part,16),self.part), :]
    def own(self):
        n=self.net
        return n.move(self.source(2*n.zl+n.c,0,self.size), self.dst.at[n.z, pl.ds(self.offset,self.size), :])
    def start(self, k):
        n=self.net
        if not hasattr(self,"zs"): self.zs={}; self.rs={}
        zl=1-n.zl if k&1 else n.zl
        self.zs[k]=n.copy(self.source(2*zl+n.c, pl.multiple_of(n.r*self.part,16), self.part), self.place(n.z,n.r), n.to_col(k))
    def forward(self, k):
        n=self.net
        self.zs[k].wait_recv()
        b=self.place(n.xor(k),n.r)
        self.rs[k]=[n.copy(b,b,n.to_r(s)) for s in range(1,n.reps)]
    def wait(self, k):
        for h in self.rs[k]: h.wait_recv()

def feature_row(half):
    j=lax.broadcasted_iota(jnp.int32,(1,half),1).astype(F32)
    freq=jnp.exp(j*(-math.log(10000.0)/half))
    zeta=jnp.log((j/half+0.4)/1.4)
    return freq,zeta

def start_kernel(reps, x_in, d_out, lens, groups, vec, wq, wk, wv, ws, wo, wg, wu, wd,
    N1, GR, XO, VEC, Q, K, V, SW, WT, GH, GI, HL, W_in, W_gu, W_o, W_d, OFF, CQ, SQ, CK, SK,
    X, G, ACC, send, recv, local):
    net=Net(reps, send, recv, local)
    r,c,x,z,zh,zl=net.r,net.c,net.x,net.z,net.zh,net.zl
    rows,width=N1.shape; B=rows//8; Dz=width//4; half=CQ.shape[1]
    kd=Q.shape[1]; vh=V.shape[1]; ff=W_gu.shape[1]//2
    net.barrier()
    def swap(src, buf):
        i=net.used; net.used+=1; j=net.used_local; net.used_local+=1
        far=pltpu.make_async_remote_copy(src, buf.at[x,z], send.at[i], recv.at[i], device_id=net.at(c=zh,z=2*c+zl), device_id_type=MESH)
        near=pltpu.make_async_copy(src, buf.at[x,z], local.at[j])
        @pl.when(c!=zh)
        def _(): far.start()
        @pl.when(c==zh)
        def _(): near.start()
        def wait():
            @pl.when(c!=zh)
            def _(): far.wait()
            @pl.when(c==zh)
            def _(): near.wait()
        return wait
    swap_x=swap(x_in,X)
    vec_own=net.move(vec, VEC.at[z])
    vec_z=[net.copy(vec,VEC.at[z],net.to_col(k)) for k in (1,2,3)]
    units=[Fetch(net,wq,W_in,0,kd,False),Fetch(net,wk,W_in,kd,kd,False),Fetch(net,wv,W_in,2*kd,vh,False),Fetch(net,ws,W_in,2*kd+vh,vh,False)]
    for u in units:
        for k in (3,2,1): u.start(k)
    swap_g=swap(d_out,G)
    owns=[u.own() for u in units]
    late=[Fetch(net,wo,W_o,0,wo.shape[0],True),Fetch(net,wd,W_d,0,wd.shape[0],True),Fetch(net,wg,W_gu,0,ff,False),Fetch(net,wu,W_gu,ff,ff,False)]
    owns+=[u.own() for u in late]
    view=lambda buf: (lambda x_,c_,zl_,h: buf.at[x_,2*c_+zl_] if h is None else buf.at[x_,2*c_+zl_,pl.ds(h*(4*B//2),4*B//2),:])
    swap_x()
    gx=Gather(net,view(X)); gx.start()
    group=2*r+zh
    slot=lax.broadcasted_iota(jnp.int32,(rows,half),0)
    off=jnp.full((rows,half),1<<20,jnp.int32); posn=slot; start=jnp.int32(0)
    OFF[...]=off
    POS=ACC.at[:,0:half]
    POS[...]=slot.astype(F32)
    def seq(i,start):
        n=jnp.where(groups[i]==group,lens[i],0)
        slot=lax.broadcasted_iota(jnp.int32,(rows,half),0)
        inside=(slot>=start)&(slot<start+n)
        OFF[...]=jnp.where(inside,start,OFF[...])
        POS[...]=jnp.where(inside,(slot-start).astype(F32),POS[...])
        return start+n
    lax.fori_loop(0,lens.shape[0],seq,jnp.int32(0))
    freq,zeta=feature_row(half)
    def table(i,_):
        s=pl.ds(pl.multiple_of(i*B,B),B)
        pos=POS[s,:]
        ang=pos*freq
        co=jnp.cos(ang); si=jnp.sin(ang)
        up=jnp.exp(pos*zeta*(1/512.0)); dn=jnp.exp(pos*zeta*(-1/512.0))
        CQ[s,:]=co*up; SQ[s,:]=si*up; CK[s,:]=co*dn; SK[s,:]=si*dn
        return 0
    lax.fori_loop(0,8,table,0)
    gx.after_z(); gx.after_x()
    swap_g()
    gx.after_diag()
    gg=Gather(net,view(G)); gg.start()
    vec_own.wait()
    for h in vec_z: h.wait_recv()
    gx.wait_c()
    def ln1(j,_):
        x_=j//(4*B//32); row=lax.rem(j,4*B//32)*32
        parts=[X[x_,f,pl.ds(pl.multiple_of(row,32),32),:].astype(F32) for f in range(4)]
        mean=sum(jnp.sum(p,axis=1,keepdims=True) for p in parts)/width
        parts=[p-mean for p in parts]
        var=sum(jnp.sum(p*p,axis=1,keepdims=True) for p in parts)/width
        inv=lax.rsqrt(var+NORM_EPS)
        for f in range(4):
            N1[pl.ds(pl.multiple_of(j*32,32),32),f*Dz:(f+1)*Dz]=(parts[f]*inv*VEC[f,0:1,:]+VEC[f,1:2,:]).astype(BF16)
        return 0
    lax.fori_loop(0,rows//32,ln1,0)
    own_rows=pl.ds(pl.multiple_of((2*c+zl)*B,B),B)
    for f in range(4):
        XO[:,f*Dz:(f+1)*Dz]=X[x,f,own_rows,:]
    for h in owns: h.wait()
    T=rows//4
    def project(zz, first):
        def tile(i,_):
            s=pl.ds(pl.multiple_of(i*T,T),T)
            a=N1[s,pl.ds(pl.multiple_of(zz*Dz,Dz),Dz)]
            p=dot_nt(a,W_in[zz])
            if first: ACC[s,:]=p
            else: ACC[s,:]+=p
            return 0
        lax.fori_loop(0,rows//T,tile,0)
    for k in (1,):
        for u in units: u.forward(k)
    gg.after_z(); gg.after_x()
    for u in units:
        for k in (2,3): u.forward(k)
    gg.after_diag()
    for u in late:
        for k in (3,2,1): u.start(k)
    for k in (1,2,3):
        for u in units: u.wait(k)
    project(z,True)
    for k in (1,2,3):
        project(net.xor(k),False)
    gg.wait_c()
    def mask(j,_):
        x_=j//4; s=pl.ds(pl.multiple_of(lax.rem(j,4)*B,B),B); d=pl.ds(pl.multiple_of(j*B,B),B)
        keep=OFF[d,0:1]<(1<<20)
        for f in range(4):
            GR[d,f*Dz:(f+1)*Dz]=jnp.where(keep,G[x_,f,s,:],jnp.zeros((),BF16))
        return 0
    lax.fori_loop(0,8,mask,0)
    def split(i,_):
        s=pl.ds(pl.multiple_of(i*B,B),B)
        for base,C,S,O in ((0,CQ,SQ,Q),(kd,CK,SK,K)):
            a=ACC[s,base:base+half]; b=ACC[s,base+half:base+kd]
            co=C[s,:]; si=S[s,:]
            O[s,0:half]=(a*co-b*si).astype(BF16)
            O[s,half:kd]=(b*co+a*si).astype(BF16)
        V[s,:]=ACC[s,2*kd:2*kd+vh].astype(BF16)
        SW[s,:]=ACC[s,2*kd+vh:]
        return 0
    lax.fori_loop(0,8,split,0)
    head=(4*x+2*zl+c).astype(F32)
    rate=jnp.log1p(-jnp.exp2(jnp.full((1,1),-5.0,F32)-head))
    gains=[jnp.where(2*zl+c==f,VEC[f,4:5,:],0.0) for f in range(4)]
    gain=sum(gains)
    for i in range(rows//T):
        s=slice(i*T,(i+1)*T); U=(i+1)*T
        scores=dot_nt(Q[s,:],K[0:U,:])
        t=lax.broadcasted_iota(jnp.int32,(T,U),0)+i*T
        u=lax.broadcasted_iota(jnp.int32,(T,U),1)
        allowed=(u<=t)&(u>=OFF[s,0:1])
        decay=jnp.where(allowed,jnp.exp((t-u).astype(F32)*rate)*(1/math.sqrt(kd)),0.0)
        WT[s,0:U]=(scores*decay).astype(BF16)
        ret=dot_nn(WT[s,0:U],V[0:U,:])
        cen=ret-jnp.mean(ret,axis=1,keepdims=True)
        inv=lax.rsqrt(jnp.mean(cen*cen,axis=1,keepdims=True)+GROUP_EPS)
        hat=cen*inv
        GH[s,:]=hat
        GI[s,:]=jnp.broadcast_to(inv,(T,half))
        sw=SW[s,:]
        HL[s,:]=(sw*jax.nn.sigmoid(sw)*(hat*gain)).astype(BF16)
        u_=late[i] if i<len(late) else None
        if u_ is not None:
            for k in (1,2,3): u_.forward(k)
    for u_ in late:
        for k in (1,2,3): u_.wait(k)
    net.finish()

def call_start(args, reps, dims):
    rows,width,kd,vh,ff,half=dims
    o=lambda s,d: jax.ShapeDtypeStruct(s,d)
    out=[o((rows,width),BF16),o((rows,width),BF16),o((rows//8,width),BF16),o((4,8,width//4),F32),
      o((rows,kd),BF16),o((rows,kd),BF16),o((rows,vh),BF16),o((rows,vh),F32),o((rows,rows),BF16),o((rows,vh),F32),o((rows,half),F32),o((rows,vh),BF16),
      o((4,2*kd+2*vh,width//4),BF16),o((4,2*ff,width//4),BF16),o((4,width//4,vh),BF16),o((4,width//4,ff),BF16),
      o((rows,half),jnp.int32)]+[o((rows,half),F32)]*4
    hbm=pl.BlockSpec(memory_space=pl.ANY); sm=pl.BlockSpec(memory_space=pltpu.SMEM); vm=pl.BlockSpec(memory_space=pltpu.VMEM)
    sems=120+40*reps
    return pl.pallas_call(functools.partial(start_kernel,reps), out_shape=out,
      in_specs=[hbm,hbm,sm,sm]+[hbm]*9, out_specs=[vm]*len(out),
      scratch_shapes=[pltpu.VMEM((2,4,rows//2,width//4),BF16),pltpu.VMEM((2,4,rows//2,width//4),BF16),pltpu.VMEM((rows,2*kd+2*vh),F32),
        pltpu.SemaphoreType.DMA((sems,)),pltpu.SemaphoreType.DMA((sems,)),pltpu.SemaphoreType.DMA((16,))],
      compiler_params=pltpu.CompilerParams(collective_id=0,has_side_effects=True,vmem_limit_bytes=62<<20),
      cost_estimate=pl.CostEstimate(flops=10**10,bytes_accessed=10**8,transcendentals=10**7),
    )(*args)


def permute(value, change, reps):
    pairs = []
    for r, c, x, zh, zl in itertools.product(range(reps), range(2), range(2), range(2), range(2)):
        r2, c2, x2, zh2, zl2 = change(r, c, x, zh, zl)
        source = ((2 * r + c) * 2 + x) * 4 + 2 * zh + zl
        target = ((2 * r2 + c2) * 2 + x2) * 4 + 2 * zh2 + zl2
        pairs.append((source, target))
    return lax.ppermute(value, AXES, pairs)


class Links:
    def __init__(self, reps):
        self.reps = reps

    def x(self, value):
        return permute(value, lambda r, c, x, zh, zl: (r, c, 1 - x, zh, zl), self.reps)

    def z(self, value):
        return permute(value, lambda r, c, x, zh, zl: (r, c, x, zh, 1 - zl), self.reps)

    def c(self, value):
        return permute(value, lambda r, c, x, zh, zl: (r, 1 - c, x, zh, zl), self.reps)

    def swap(self, value):
        return permute(value, lambda r, c, x, zh, zl: (r, zh, x, c, zl), self.reps)

    def col(self, value, k):
        return permute(
            value, lambda r, c, x, zh, zl: (r, c, x, zh ^ (k >> 1), zl ^ (k & 1)), self.reps
        )

    def r(self, value, k):
        return permute(
            value, lambda r, c, x, zh, zl: ((r + k) % self.reps, c, x, zh, zl), self.reps
        )

    def home(self, value, k):
        def change(r, c, x, zh, zl):
            target = (2 * c + zl) ^ k
            return (r, zh, x, target >> 1, target & 1)

        return permute(value, change, self.reps)


def slot_layout(seq_lens, seq_groups, group_index, slot_ids):
    is_mine = seq_groups == group_index
    own_lengths = jnp.where(is_mine, seq_lens, 0)
    starts = jnp.cumsum(own_lengths) - own_lengths
    inside = (
        is_mine[None, :]
        & (slot_ids[:, None] >= starts[None, :])
        & (slot_ids[:, None] < (starts + own_lengths)[None, :])
    )
    is_valid = jnp.any(inside, axis=1)
    number = jnp.arange(seq_lens.shape[0], dtype=jnp.int32)
    found = jnp.sum(jnp.where(inside, number[None, :], 0), axis=1)
    segment = jnp.where(is_valid, found, -1)
    offsets = jnp.sum(jnp.where(inside, starts[None, :], 0), axis=1)
    position = (slot_ids - offsets).astype(F32)
    return (segment, position)


def rotate_scale(values, position, direction):
    half_width = values.shape[-1] // 2
    pair_index = jnp.arange(half_width, dtype=F32)
    frequency = jnp.exp(pair_index * (-math.log(10000.0) / half_width))
    zeta_base = (pair_index / half_width + 0.4) / 1.4
    angles = position[:, None] * frequency[None, :]
    growth = jnp.exp(direction / 512.0 * position[:, None] * jnp.log(zeta_base)[None, :])
    cos_scaled = jnp.cos(angles) * growth
    sin_scaled = jnp.sin(angles) * growth
    first_half = values[:, :half_width]
    second_half = values[:, half_width:]
    return jnp.concatenate(
        [
            first_half * cos_scaled - second_half * sin_scaled,
            second_half * cos_scaled + first_half * sin_scaled,
        ],
        axis=1,
    )


def head_mix(retained, gate_raw, gain_vec):
    average = jnp.mean(retained, axis=1, keepdims=True)
    centered = retained - average
    variance = jnp.mean(centered * centered, axis=1, keepdims=True)
    normed = centered * lax.rsqrt(variance + GROUP_EPS) * gain_vec
    return jax.nn.silu(gate_raw) * normed


def gelu_mix(gate_raw, up_raw):
    return jax.nn.gelu(gate_raw, approximate=True) * up_raw


def contract_last(left, right):
    return lax.dot_general(left, right, (((1,), (1,)), ((), ())), preferred_element_type=F32)


def contract_first(left, right):
    return lax.dot_general(left, right, (((0,), (0,)), ((), ())), preferred_element_type=F32)


def dot(left, right):
    return jnp.dot(left, right, preferred_element_type=F32)


def center(values):
    average = jnp.mean(values, axis=1, keepdims=True)
    shifted = values - average
    inverse = lax.rsqrt(jnp.mean(shifted * shifted, axis=1, keepdims=True) + NORM_EPS)
    return (shifted * inverse, inverse)


def norm_backward(d_normed, centered, inverse, gain_vec):
    d_gain = jnp.sum(d_normed * centered, axis=0)
    d_bias = jnp.sum(d_normed, axis=0)
    d_scaled = d_normed * gain_vec
    mean_first = jnp.mean(d_scaled, axis=1, keepdims=True)
    mean_cross = jnp.mean(d_scaled * centered, axis=1, keepdims=True)
    return (inverse * (d_scaled - mean_first - centered * mean_cross), d_gain, d_bias)


def scaled_decay(segment, slots, log_rate, width):
    distance = slots[:, None] - slots[None, :]
    allowed = (
        (segment[:, None] == segment[None, :]) & (segment[:, None] >= 0) & (distance >= 0)
    )
    steps_back = jnp.maximum(distance, 0).astype(F32)
    return jnp.where(allowed, jnp.exp(steps_back * log_rate), 0.0) / math.sqrt(width)


def gather_rows(own, links):
    rows, width = own.shape
    half = width // 2
    first, second = (own[:, :half], own[:, half:])
    first_z = links.z(first)
    second_x = links.x(second)
    first_pair = jnp.stack([first, first_z])
    second_pair = jnp.stack([second, second_x])
    first_x = links.x(first_pair)
    second_z = links.z(second_pair)
    first_all = jnp.stack([first_pair, first_x])
    second_all = jnp.stack([second_pair, second_z], axis=1)
    mine = jnp.concatenate([first_all, second_all], axis=-1)
    other = links.c(mine)
    return jnp.stack([mine, other], axis=1).reshape(8 * rows, width)


def scatter_rows(half_of, links, width):
    arriving = links.c(half_of(1))
    chip_sum = half_of(0).astype(F32) + arriving.astype(F32)
    half = width // 2
    first, second = (chip_sum[..., :half], chip_sum[..., half:])
    first = first[0] + links.x(first[1].astype(BF16)).astype(F32)
    second = second[:, 0] + links.z(second[:, 1].astype(BF16)).astype(F32)
    first = first[0] + links.z(first[1].astype(BF16)).astype(F32)
    second = second[0] + links.x(second[1].astype(BF16)).astype(F32)
    return jnp.concatenate([first, second], axis=-1)


def half_rows(value, jc):
    rows = value.shape[0] // 8
    return value.reshape(2, 2, 2 * rows, -1)[:, jc].reshape(4 * rows, -1)


def partial_product(left, weight, links, transposed):
    width = weight.shape[0] if transposed else weight.shape[1]
    rows = left.shape[0] // 8

    def half_of(jc):
        part = half_rows(left, jc)
        product = contract_last(part, weight) if transposed else dot(part, weight)
        return product.astype(BF16).reshape(2, 2, rows, width)

    return scatter_rows(half_of, links, width)


def gather_block(block, links, c, zl):
    block_rows, block_width = block.shape
    half = block_rows // 2
    first, second = (block[:half], block[half:])
    first_z = links.z(first)
    second_x = links.x(second)
    first_pair = jnp.stack([first, first_z])
    second_pair = jnp.stack([second, second_x])
    first_x = links.x(first_pair)
    second_z = links.z(second_pair)
    first_all = jnp.stack([first_pair, first_x])
    second_all = jnp.stack([second_pair, second_z], axis=1)
    mine = jnp.concatenate([first_all, second_all], axis=2)
    other = links.c(mine)
    both = jnp.stack([mine, other])
    columns = []
    for fc, fz in itertools.product(range(2), range(2)):
        piece = lax.dynamic_index_in_dim(both, c ^ fc, 0, keepdims=False)
        columns.append(lax.dynamic_index_in_dim(piece, zl ^ fz, 1, keepdims=False))
    whole = jnp.concatenate(columns, axis=-1)
    whole = whole.reshape(2, 4, block_rows // 4, -1)
    own = 2 * c + zl
    blocks = [lax.dynamic_index_in_dim(whole, own ^ j, 1, keepdims=True) for j in range(4)]
    return jnp.concatenate(blocks, axis=1).reshape(2 * block_rows, -1)


def send_home(own, links, c, zl, z):
    rows, width = own.shape
    part = width // 4
    low = own.astype(BF16)
    out = jnp.zeros((4 * rows, part), F32)
    for k in range(4):
        piece = lax.dynamic_slice_in_dim(low, ((2 * c + zl) ^ k) * part, part, 1)
        got = links.home(piece, k).astype(F32)
        out = lax.dynamic_update_slice_in_dim(out, got, (z ^ k) * rows, 0)
    return out


def head_rows(weight, head):
    size = weight.shape[0] // 4
    return lax.dynamic_slice_in_dim(weight, head * size, size, 0)


def head_columns(weight, head):
    size = weight.shape[1] // 4
    return lax.dynamic_slice_in_dim(weight, head * size, size, 1)


def fetch_rows(weights, links, c, r, z):
    reps = links.reps
    width = weights[0].shape[1]
    part = width // reps

    def stacked(k):
        head = ((z ^ k) & 1) * 2 + c
        return jnp.concatenate([head_rows(weight, head) for weight in weights], axis=0)

    own = stacked(0)
    out = jnp.zeros((own.shape[0], 4 * width), BF16)
    out = lax.dynamic_update_slice_in_dim(out, own, z * width, 1)
    for k in (2, 3, 1):
        piece = lax.dynamic_slice_in_dim(stacked(k), r * part, part, 1)
        got = links.col(piece, k)
        out = lax.dynamic_update_slice_in_dim(out, got, (z ^ k) * width + r * part, 1)
        for step in range(1, reps):
            more = links.r(got, step)
            place = (z ^ k) * width + ((r - step) % reps) * part
            out = lax.dynamic_update_slice_in_dim(out, more, place, 1)
    return out


def fetch_columns(weight, links, c, r, z):
    reps = links.reps
    height = weight.shape[0]
    part = height // reps
    own = head_columns(weight, (z & 1) * 2 + c)
    out = jnp.zeros((4 * height, own.shape[1]), BF16)
    out = lax.dynamic_update_slice_in_dim(out, own, z * height, 0)
    for k in (2, 3, 1):
        rows = lax.dynamic_slice_in_dim(weight, r * part, part, 0)
        got = links.col(head_columns(rows, ((z ^ k) & 1) * 2 + c), k)
        out = lax.dynamic_update_slice_in_dim(out, got, (z ^ k) * height + r * part, 0)
        for step in range(1, reps):
            more = links.r(got, step)
            place = (z ^ k) * height + ((r - step) % reps) * part
            out = lax.dynamic_update_slice_in_dim(out, more, place, 0)
    return out


def reduce_grad(pieces, links, c, r, z):
    reps = links.reps
    total = lax.dynamic_index_in_dim(pieces, r, 0, keepdims=False).astype(F32)
    for step in range(1, reps):
        outgoing = lax.dynamic_index_in_dim(pieces, (r + step) % reps, 0, keepdims=False)
        total = total + links.r(outgoing, step).astype(F32)
    low = total.astype(BF16)

    def block(k):
        return lax.dynamic_index_in_dim(low, z ^ k, 0, keepdims=False)

    arrived = [block(0)] + [links.col(block(k), k) for k in (1, 2, 3)]
    same = (arrived[0].astype(F32) + arrived[2].astype(F32)).astype(BF16)
    crossed = (arrived[1].astype(F32) + arrived[3].astype(F32)).astype(BF16)
    is_low = (z & 1) == 0
    heads = jnp.stack([jnp.where(is_low, same, crossed), jnp.where(is_low, crossed, same)])
    gathered = jnp.zeros((reps,) + heads.shape, BF16)
    gathered = lax.dynamic_update_index_in_dim(gathered, heads, r, 0)
    for step in range(1, reps):
        more = links.r(heads, step)
        gathered = lax.dynamic_update_index_in_dim(gathered, more, (r - step) % reps, 0)
    other = links.c(gathered)
    first = jnp.where(c == 0, gathered, other)
    second = jnp.where(c == 0, other, gathered)
    both = jnp.stack([first, second])
    return both


def row_grads(grad, counts, links, c, r, z):
    reps = links.reps
    outs, inputs = grad.shape
    part = inputs // 4 // reps
    pieces = grad.astype(BF16).reshape(outs, 4, reps, part).transpose(2, 1, 0, 3)
    both = reduce_grad(pieces, links, c, r, z)
    ordered = both.transpose(2, 0, 3, 1, 4).reshape(4, outs, inputs // 4)
    results = []
    offset = 0
    for count in counts:
        piece = ordered[:, offset : offset + count]
        results.append(piece.reshape(4 * count, inputs // 4).astype(F32))
        offset += count
    return results


def column_grad(grad, links, c, r, z):
    reps = links.reps
    outs, inputs = grad.shape
    part = outs // 4 // reps
    pieces = grad.astype(BF16).reshape(4, reps, part, inputs).transpose(1, 0, 2, 3)
    both = reduce_grad(pieces, links, c, r, z)
    return both.transpose(1, 3, 2, 0, 4).reshape(outs // 4, 4 * inputs).astype(F32)


def body(
    x_in,
    seq_lens,
    seq_groups,
    ln1_gain,
    ln1_bias,
    w_query,
    w_key,
    w_value,
    w_swish,
    gn_gain,
    w_out,
    ln2_gain,
    ln2_bias,
    w_mlp_gate,
    w_mlp_up,
    w_down,
    d_out,
):
    reps = lax.axis_size("dp") // 2
    links = Links(reps)
    dp_at = lax.axis_index("dp")
    r, c = (dp_at // 2, dp_at % 2)
    x = lax.axis_index("row")
    z = lax.axis_index("col")
    zh, zl = (z // 2, z % 2)
    block_rows, block_width = x_in.shape
    rows = block_rows // 4
    width = block_width * 4
    key_width = w_query.shape[0] // 4
    value_width = w_value.shape[0] // 4
    ffn_width = w_mlp_gate.shape[0] // 4
    head_at = 2 * zl + c

    vec = jnp.zeros((8, block_width), F32).at[:5].set(jnp.stack([ln1_gain, ln1_bias, ln2_gain, ln2_bias, gn_gain]))
    out = call_start((x_in, d_out, seq_lens, seq_groups, vec, w_query, w_key, w_value, w_swish, w_out, w_mlp_gate, w_mlp_up, w_down), reps, (rows*8, width, key_width, value_width, ffn_width, key_width//2))
    (n1, gr, xo, vv, q, k, v, sw, wt, gh, gi, hl, w_in, w_gu, w_o, w_d, off, cq, sq, ck, sk) = out
    blocks = jnp.arange(8, dtype=jnp.int32)
    natural = (x ^ (blocks >> 2)) * 4 + (c ^ ((blocks >> 1) & 1)) * 2 + (zl ^ (blocks & 1))
    rel = lambda a: jnp.take(a.reshape((8, rows) + a.shape[1:]), natural, axis=0).reshape(a.shape)
    gain1, bias1, gain2, bias2 = (vv[:, i].reshape(-1) for i in range(4))
    gain_vec = lax.dynamic_slice_in_dim(vv[:, 4].reshape(-1), head_at * value_width, value_width, 0)
    x_own = xo.astype(F32)
    normed1 = rel(n1); query_low = rel(q); key_low = rel(k); value_low = rel(v)
    weight_in = w_in.transpose(1, 0, 2).reshape(w_in.shape[1], -1)
    weight_ffn = w_gu.transpose(1, 0, 2).reshape(w_gu.shape[1], -1)
    weight_out = w_o.reshape(-1, value_width)
    weight_down = w_d.reshape(-1, ffn_width)
    slots = (natural[:, None] * rows + jnp.arange(rows, dtype=jnp.int32)[None, :]).reshape(-1)
    segment, position = slot_layout(seq_lens, seq_groups, 2 * r + zh, slots)
    log_rate = jnp.log1p(-jnp.exp2(-5.0 - (4 * x + head_at).astype(F32)))
    decay = scaled_decay(segment, slots, log_rate, key_width)
    _, query_pull = jax.vjp(functools.partial(rotate_scale, position=position, direction=1.0), jnp.zeros(q.shape, F32))
    _, key_pull = jax.vjp(functools.partial(rotate_scale, position=position, direction=-1.0), jnp.zeros(q.shape, F32))
    weights = (contract_last(query_low, key_low) * decay).astype(BF16)
    retained = dot(weights, value_low)
    mixed_heads, mix_pull = jax.vjp(head_mix, retained, rel(sw), gain_vec)
    heads_low = rel(hl)
    attn_own = partial_product(heads_low, weight_out, links, True)
    resid = x_own + attn_own
    centered2, inverse2 = center(resid)
    normed2 = gather_rows((centered2 * gain2 + bias2).astype(BF16), links)
    gate_up = contract_last(normed2, weight_ffn)
    hidden_value, hidden_pull = jax.vjp(gelu_mix, gate_up[:, :ffn_width], gate_up[:, ffn_width:])
    hidden_low = hidden_value.astype(BF16)

    grad_all = rel(gr)
    grad_own = grad_all[:rows].astype(F32)
    d_hidden = dot(grad_all, weight_down)
    d_gate, d_up = hidden_pull(d_hidden)
    grad_ffn = jnp.concatenate([d_gate, d_up], axis=1).astype(BF16)
    d_normed2 = partial_product(grad_ffn, weight_ffn, links, False)
    d_w_down = column_grad(contract_first(grad_all, hidden_low), links, c, r, z)
    ffn_own = partial_product(hidden_low, weight_down, links, True)
    y_out = send_home(resid + ffn_own, links, c, zl, z)
    d_w_mlp_gate, d_w_mlp_up = row_grads(
        contract_first(grad_ffn, normed2), (ffn_width, ffn_width), links, c, r, z
    )
    d_resid_part, d_ln2_gain, d_ln2_bias = norm_backward(d_normed2, centered2, inverse2, gain2)
    d_resid = grad_own + d_resid_part
    d_resid_all = gather_rows(d_resid.astype(BF16), links)
    d_heads = dot(d_resid_all, weight_out)
    d_w_out = column_grad(contract_first(d_resid_all, heads_low), links, c, r, z)
    d_retained, d_swish, d_gn_gain = mix_pull(d_heads)
    d_retained = d_retained.astype(BF16)
    d_scores = (contract_last(d_retained, value_low) * decay).astype(BF16)
    d_query = dot(d_scores, key_low)
    d_key = contract_first(d_scores, query_low)
    d_value = contract_first(weights, d_retained)
    (d_query_raw,) = query_pull(d_query)
    (d_key_raw,) = key_pull(d_key)
    grad_attn = jnp.concatenate([d_query_raw, d_key_raw, d_value, d_swish], axis=1).astype(BF16)
    d_normed1 = partial_product(grad_attn, weight_in, links, False)
    (d_w_swish,) = row_grads(
        contract_first(grad_attn[:, 2 * key_width + value_width :], normed1),
        (value_width,), links, c, r, z,
    )
    d_w_query, d_w_key, d_w_value = row_grads(
        contract_first(grad_attn[:, : 2 * key_width + value_width], normed1),
        (key_width, key_width, value_width), links, c, r, z,
    )
    centered1, inverse1 = center(x_own)
    d_input_part, d_ln1_gain, d_ln1_bias = norm_backward(d_normed1, centered1, inverse1, gain1)
    d_x_in = send_home(d_resid + d_input_part, links, c, zl, z)

    gn_places = jnp.zeros((2, 4, value_width), F32)
    gn_places = lax.dynamic_update_slice(gn_places, d_gn_gain[None, None], (x, head_at, 0))
    summed = lax.psum(
        jnp.concatenate(
            [d_ln1_gain, d_ln1_bias, d_ln2_gain, d_ln2_bias, gn_places.reshape(-1)]
        ).reshape(-1, width),
        AXES,
    )
    mine = lax.dynamic_slice_in_dim(summed[:4], z * block_width, block_width, 1)
    d_gn_gain = lax.dynamic_slice(
        summed[4:].reshape(8, value_width), (4 * x + z, 0), (1, value_width)
    ).reshape(-1)
    return (
        y_out,
        d_x_in,
        mine[0],
        mine[1],
        d_w_query,
        d_w_key,
        d_w_value,
        d_w_swish,
        d_gn_gain,
        d_w_out,
        mine[2],
        mine[3],
        d_w_mlp_gate,
        d_w_mlp_up,
        d_w_down,
    )


def solution(mesh):
    return jax.shard_map(
        body,
        mesh=mesh,
        in_specs=(
            P(("dp", "row"), "col"),
            P(),
            P(),
            P("col"),
            P("col"),
            P("row", "col"),
            P("row", "col"),
            P("row", "col"),
            P("row", "col"),
            P(("row", "col")),
            P("col", "row"),
            P("col"),
            P("col"),
            P("row", "col"),
            P("row", "col"),
            P("col", "row"),
            P(("dp", "row"), "col"),
        ),
        out_specs=(
            P(("dp", "row"), "col"),
            P(("dp", "row"), "col"),
            P("col"),
            P("col"),
            P("row", "col"),
            P("row", "col"),
            P("row", "col"),
            P("row", "col"),
            P(("row", "col")),
            P("col", "row"),
            P("col"),
            P("col"),
            P("row", "col"),
            P("row", "col"),
            P("col", "row"),
        ),
        check_vma=False,
    )
```
